32 devices in a mesh: groups: 2 (over y), db: 4 (over z), sub: 2 (over x), rep: 2 (over core).
Axes of the slice: x: 2, y: 2, z: 4, core: 2. Of those that a mesh axis runs over, the one named last changes fastest.
Arguments:
- query_pooled: bfloat16 [128, 1280], P(('groups', 'db')), parts along dimension 0, may hold values from -48 to 48
- db_pooled: bfloat16 [8192, 1280], P(('groups', 'db', 'sub', 'rep')), parts along dimension 0, may hold values from -48 to 48
- query_res: bfloat16 [64, 64, 1280], P(('groups', 'db', 'sub', 'rep')), parts along dimension 0, may hold values from -48 to 48
- query_len: int32 [64], P(('groups', 'db', 'sub', 'rep')), parts along dimension 0, may hold values from 1 to 64, 1280 in all
- db_res: bfloat16 [128, 64, 1280], P(('groups', 'db', 'sub', 'rep')), parts along dimension 0, may hold values from -48 to 48
- db_len: int32 [128], P(('groups', 'db', 'sub', 'rep')), parts along dimension 0, may hold values from 1 to 64, 2560 in all
- cand_seq: int32 [128], P(('groups', 'db', 'sub', 'rep')), parts along dimension 0, may hold values from 0 to 3
- cand_dest: int32 [128, 1], P(('groups', 'db', 'sub', 'rep')), parts along dimension 0, may hold values from 0 to 3; in each aligned block of 4 rows (0 to 3, 4 to 7, ...) at most 2 rows name the same one
- cand_query: int32 [128], P(('groups', 'db', 'sub', 'rep')), parts along dimension 0, may hold values from 0 to 1
Outputs:
- coarse: float32 [128], P(('groups', 'db')), parts along dimension 0
- align_score: float32 [128], P(('groups', 'db', 'sub', 'rep')), parts along dimension 0
The draws below stay inside these ranges and needn't reach their ends.
There are 2 independent parts, one for each index of `groups`. The reference program is written for one: setup_inputs(seed, part) draws one part's arguments, and reference() takes and returns one part's arrays. A program takes and returns all parts, laid end to end along the dimension named above; each array names one. Nothing has to cross between parts.
Inputs may be any that keep to these rules, and one draw needn't show every extreme that they name: `cand_dest`: among the 4 candidates of one device, at most 2 name the same db index, and in every draw some device has exactly 2 naming one index. `query_len`: in each part along groups the 32 lengths sum to 1280, and some query has exactly 64 residues. `db_len`: in each part along groups the 64 lengths sum to 2560, and some sequence has exactly 64 residues.
All inputs are finite; a program needn't handle non-finite values.
Results may differ from the reference program's by a relative error of at most 0.0003.
Values may be sent and summed in bfloat16 or wider, within the bound.
A program may use at most 128 MiB of HBM per device.

```python
import math
import jax
import jax.numpy as jnp
import numpy as np
from jax import lax

D = 1280
TD = 4
QR = 2
LMAX = 64
CAP = 2
CPD = 4
NQP = 64
NDBP = 4096
NT = 64
NQ = 32
NCAND = 64
N_DB = 4
N_SUB = 2
N_REP = 2


def noise_rows(key, salt, shape):
    return jnp.clip(jax.random.normal(jax.random.fold_in(key, salt), shape, jnp.float32), -4.0, 4.0)


def query_like(key, salt, shape):
    values = noise_rows(key, salt, shape)
    return jnp.clip(values, -48.0, 48.0)


def base_like(key, salt, shape):
    values = noise_rows(key, salt, shape)
    return jnp.clip(values, -48.0, 48.0)


def draw_query_pooled(key, part):
    return query_like(key, 101, (NQP, D)).astype(jnp.bfloat16)


def draw_db_pooled(key, part):
    return base_like(key, 201, (NDBP, D)).astype(jnp.bfloat16)


def draw_query_res(key, part):
    return query_like(key, 301, (NQ, LMAX, D)).astype(jnp.bfloat16)


def draw_db_res(key, part):
    return base_like(key, 401, (NT, LMAX, D)).astype(jnp.bfloat16)


def plant(entries, rng, smallest, top_value):
    spot = [jax.random.randint(jax.random.fold_in(rng, axis), (), 0, length) for axis, length in enumerate(entries.shape)]
    widest = entries.shape.index(max(entries.shape))
    next_to = spot[:widest] + [(spot[widest] + 1) % entries.shape[widest]] + spot[widest + 1:]
    return entries.at[tuple(spot)].set(smallest).at[tuple(next_to)].set(top_value)


def split_up(number_of, total, limit, lean):
    loads = [(1 << 20) // math.isqrt(grade ** lean) + 1 for grade in range(2, number_of + 1)]
    rest, given = total - limit - (number_of - 1), [1] * (number_of - 1)
    while rest > 0:
        movable = [i for i in range(number_of - 1) if given[i] < limit]
        whole, budget = sum([loads[i] for i in movable]), rest
        for i in movable:
            more = min(limit - given[i], max(1, budget * loads[i] // whole), rest)
            given[i] = given[i] + more
            rest = rest - more
    return np.array([limit] + given)


def uneven_parts(key, count, total, bound, lean):
    if count == 2:
        one = jax.random.randint(key, (), max(1, total - bound), min(bound, total - 1) + 1)
        return jnp.stack([one, total - one])
    lengths = jnp.asarray(split_up(count, total, bound, lean), jnp.int32)
    twos = (count - 1) // 2
    giver, taker = lengths[1:1 + 2 * twos:2], lengths[2:2 + 2 * twos:2]
    room = jnp.minimum(giver - 1, bound - taker)
    moved = jax.random.randint(jax.random.fold_in(key, 1), (twos,), 0, 1 << 20) % (room + 1)
    lengths = lengths.at[1:1 + 2 * twos:2].set(giver - moved).at[2:2 + 2 * twos:2].set(taker + moved)
    return lengths[jax.random.permutation(jax.random.fold_in(key, 2), count)]


def routed_block(stream_key, own, number, rows, count, top, reach, lean):
    ranking = jax.random.permutation(stream_key, count)
    crowded, usual = portions_of(count, rows * top, reach, lean, True), portions_of(count, rows * top, reach, lean, False)
    places = jnp.arange(count)

    def named(lengths, turn):
        used = int((lengths > 0).sum())
        fixed = max(1, used // 4)
        passed = fixed + (places - fixed + turn * (used - fixed)) % max(1, count - fixed)
        return jnp.zeros((count,), jnp.int32).at[ranking[jnp.where(places < fixed, places, passed)]].set(jnp.asarray(lengths, jnp.int32))

    lengths = jnp.where(number % 4 == 0, named(crowded, number // 4), named(usual, number - number // 4 - 1))
    mixed = jax.random.permutation(jax.random.fold_in(own, 3), count)
    source_of, sink = mixed[0:count // 2 * 2:2], mixed[1:count // 2 * 2:2]
    slack = jnp.minimum(lengths[source_of] - 1, reach - lengths[sink]) // 2
    slack = jnp.where((source_of == ranking[0]) | (sink == ranking[0]) | (lengths[sink] == 0), 0, jnp.maximum(slack, 0))
    passed = jax.random.randint(jax.random.fold_in(own, 4), (count // 2,), 0, 1 << 20) % (slack + 1)
    lengths = lengths.at[source_of].add(-passed).at[sink].add(passed)
    labels = jnp.searchsorted(jnp.cumsum(lengths), jnp.arange(rows * top), side="right").astype(jnp.int32)
    grid = labels.reshape(top, rows).T
    grid = grid[jax.random.permutation(jax.random.fold_in(own, 1), rows)]
    turn = jax.random.randint(jax.random.fold_in(own, 2), (rows, 1), 0, top)
    return jnp.take_along_axis(grid, (jnp.arange(top)[None, :] + turn) % top, axis=1)


def portions_of(amount, total, reach, slope, full):
    weights = [(1 << 20) // math.isqrt(grade ** slope) + 1 for grade in range(1, amount + 1)]
    largest = reach if full else min(reach, max(-(-total // amount), total * weights[0] // sum(weights)))
    least = 1 if total - largest >= amount - 1 else 0
    counts, rest = [largest] + [least] * (amount - 1), total - largest - least * (amount - 1)
    while rest > 0:
        movable = [i for i in range(1, amount) if counts[i] < largest] or [i for i in range(1, amount) if counts[i] < reach]
        mass, remaining = sum([weights[i] for i in movable]), rest
        for i in movable:
            more = min(reach - counts[i], max(1, remaining * weights[i] // mass), rest)
            counts[i] = counts[i] + more
            rest = rest - more
    return np.array(counts)


def setup_inputs(seed: int = 0, part: int = 0) -> dict:
    keys = jax.random.split(jax.random.key(seed), 10)
    own_keys = jax.random.split(jax.random.fold_in(keys[9], part), 10)
    query_pooled = draw_query_pooled(jax.random.fold_in(jax.random.fold_in(keys[9], part), 71), part)
    db_pooled = draw_db_pooled(jax.random.fold_in(jax.random.fold_in(keys[9], part), 71), part)
    query_res = draw_query_res(jax.random.fold_in(jax.random.fold_in(keys[9], part), 71), part)
    query_len = uneven_parts(own_keys[3], NQ, NQ * LMAX * 5 // 8, LMAX, 1).astype(jnp.int32)
    db_res = draw_db_res(jax.random.fold_in(jax.random.fold_in(keys[9], part), 71), part)
    db_len = uneven_parts(own_keys[5], NT, NT * LMAX * 5 // 8, LMAX, 1).astype(jnp.int32)
    cand_seq = plant(jax.random.randint(own_keys[6], (NCAND,), 0, TD), jax.random.fold_in(own_keys[6], 1), 0, TD - 1).astype(jnp.int32)
    cand_dest_keys = jax.random.split(jax.random.fold_in(own_keys[7], 1), NCAND // CPD)
    cand_dest_turns = jax.random.permutation(jax.random.fold_in(own_keys[7], 3), NCAND // CPD)
    cand_dest = jax.vmap(lambda own, number: routed_block(jax.random.fold_in(own_keys[7], 2), own, number, CPD, N_DB, 1, CAP, 2))(cand_dest_keys, cand_dest_turns).reshape((NCAND, 1))
    cand_query = plant(jax.random.randint(own_keys[8], (NCAND,), 0, QR), jax.random.fold_in(own_keys[8], 1), 0, QR - 1).astype(jnp.int32)
    return dict(query_pooled=query_pooled, db_pooled=db_pooled, query_res=query_res, query_len=query_len, db_res=db_res, db_len=db_len, cand_seq=cand_seq, cand_dest=cand_dest, cand_query=cand_query)


def join_stats(first, second):
    highest = jnp.maximum(first[0], second[0])
    summed = first[1] * jnp.exp(first[0] - highest) + second[1] * jnp.exp(second[0] - highest)
    return highest, summed


def soft_align(queries, blocks, query_lengths, block_lengths):
    factor = D ** -0.5
    similar = jnp.einsum("nid,njd->nij", queries.astype(jnp.float32), blocks.astype(jnp.float32), precision=lax.Precision.HIGHEST) * factor
    row_index = lax.broadcasted_iota(jnp.int32, similar.shape, 1)
    column_index = lax.broadcasted_iota(jnp.int32, similar.shape, 2)
    rows_valid = row_index < query_lengths[:, None, None]
    columns_valid = column_index < block_lengths[:, None, None]
    across = jnp.where(columns_valid, similar, -1e30)
    across_top = jnp.max(across, axis=2, keepdims=True)
    across_weight = jnp.where(columns_valid, jnp.exp(across - across_top), 0.0)
    across_weight = across_weight / jnp.sum(across_weight, axis=2, keepdims=True)
    down = jnp.where(rows_valid, similar, -1e30)
    down_top = jnp.max(down, axis=1, keepdims=True)
    down_weight = jnp.where(rows_valid, jnp.exp(down - down_top), 0.0)
    down_weight = down_weight / jnp.sum(down_weight, axis=1, keepdims=True)
    both_valid = rows_valid & columns_valid
    row_part = jnp.sum(jnp.where(both_valid, across_weight * similar, 0.0), axis=(1, 2))
    column_part = jnp.sum(jnp.where(both_valid, down_weight * similar, 0.0), axis=(1, 2))
    return 0.5 * row_part / query_lengths.astype(jnp.float32) + 0.5 * column_part / block_lengths.astype(jnp.float32)


def reference(query_pooled, db_pooled, query_res, query_len, db_res, db_len, cand_seq, cand_dest, cand_query):
    factor = D ** -0.5
    devices = N_DB * N_SUB * N_REP
    slabs = db_pooled.reshape(devices, -1, D)
    queries = query_pooled.astype(jnp.float32)

    def visit(carry, slab):
        similar = lax.dot_general(queries, slab.astype(jnp.float32), (((1,), (1,)), ((), ())), precision=lax.Precision.HIGHEST) * factor
        slab_top = jnp.max(similar, axis=1)
        slab_sum = jnp.sum(jnp.exp(similar - slab_top[:, None]), axis=1)
        return join_stats(carry, (slab_top, slab_sum)), None

    initial = (jnp.full((NQP,), -jnp.inf, jnp.float32), jnp.zeros((NQP,), jnp.float32))
    (highest, summed), _ = lax.scan(visit, initial, slabs)
    coarse = highest + jnp.log(summed)

    device_ids = jnp.arange(NCAND, dtype=jnp.int32) // CPD
    sub_ids = (device_ids // N_REP) % N_SUB
    rep_ids = device_ids % N_REP
    query_ids = (((cand_dest[:, 0] * N_SUB + sub_ids) * N_REP + rep_ids) * QR + cand_query).astype(jnp.int32)
    seq_ids = (device_ids * TD + cand_seq).astype(jnp.int32)

    def pairs(both_ids):
        query_part, seq_part = both_ids
        return soft_align(query_res[query_part], db_res[seq_part], query_len[query_part], db_len[seq_part])

    scores = lax.map(pairs, (query_ids.reshape(devices, CPD), seq_ids.reshape(devices, CPD)))
    return coarse, scores.reshape(-1)
```

```python
import functools

import jax
import jax.numpy as jnp
from jax import lax
from jax.experimental import pallas as pl
from jax.experimental.pallas import tpu as pltpu
from jax.sharding import PartitionSpec as P

MESH = pl.DeviceIdType.MESH
LANES = 128


def fold(pieces):
    top = functools.reduce(jnp.maximum, [p[0] for p in pieces])
    total = sum(p[1] * jnp.exp(p[0] - top) for p in pieces)
    return top, total


def align(query, block, lq_row, lt, factor):
    similar = lax.dot_general(
        query, block, (((1,), (1,)), ((), ())), preferred_element_type=jnp.float32
    ) * factor
    rows = lax.broadcasted_iota(jnp.int32, similar.shape, 0) < lq_row[:, : similar.shape[1]]
    columns = lax.broadcasted_iota(jnp.int32, similar.shape, 1) < lt
    across = jnp.where(columns, similar, -1e30)
    weight = jnp.where(columns, jnp.exp(across - jnp.max(across, axis=1, keepdims=True)), 0.0)
    row_part = jnp.sum(weight * similar, axis=1, keepdims=True) / jnp.sum(
        weight, axis=1, keepdims=True
    )
    row_part = jnp.sum(jnp.where(rows[:, :1], row_part, 0.0), axis=0, keepdims=True)
    down = jnp.where(rows, similar, -1e30)
    weight = jnp.where(rows, jnp.exp(down - jnp.max(down, axis=0, keepdims=True)), 0.0)
    column_part = jnp.sum(weight * similar, axis=0, keepdims=True) / jnp.sum(
        weight, axis=0, keepdims=True
    )
    column_part = jnp.sum(jnp.where(columns[:1], column_part, 0.0), axis=1, keepdims=True)
    lq = lq_row[:, :1].astype(jnp.float32)
    return 0.5 * row_part / lq + 0.5 * column_part / lt.astype(jnp.float32)


def kernel(
    n, n_sub, n_rep,
    qp_ref, dbp_hbm, qres_hbm, qlen_ref, dbres_hbm, dblen_ref, seq_ref, dest_ref, cq_ref,
    coarse_ref, score_ref,
    qp_all, dbp, dbres, res_all, len_all, stat, stat_db, stat_node,
    local_sem, qp_send, qp_recv, len_send, len_recv, res_send, res_recv,
    a_send, a_recv, b_send, b_recv,
):
    db, sub, rep = lax.axis_index("db"), lax.axis_index("sub"), lax.axis_index("rep")
    node = n_sub * n_rep
    spot = sub * n_rep + rep
    per_owner, width = qp_ref.shape
    held = qres_hbm.shape[0]
    factor = width ** (-0.5)

    def on_line(i):
        return lax.rem(db + i, n)

    def in_node(i):
        other = lax.rem(spot + i, node)
        return other, {"sub": other // n_rep, "rep": lax.rem(other, n_rep)}

    local = [
        pltpu.make_async_copy(qres_hbm, res_all.at[pl.ds(db * held, held)], local_sem.at[0]),
        pltpu.make_async_copy(dbp_hbm, dbp, local_sem.at[1]),
        pltpu.make_async_copy(dbres_hbm, dbres, local_sem.at[2]),
    ]
    for copy in local:
        copy.start()
    barrier = pltpu.get_barrier_semaphore()
    for i in range(1, n):
        pl.semaphore_signal(barrier, inc=1, device_id={"db": on_line(i)}, device_id_type=MESH)
    for i in range(1, node):
        pl.semaphore_signal(barrier, inc=1, device_id=in_node(i)[1], device_id_type=MESH)
    qp_all[db] = qp_ref[...]
    for q in range(held):
        len_all[db * held + q] = jnp.full(len_all.shape[1:], qlen_ref[q], jnp.int32)
    pl.semaphore_wait(barrier, n - 1 + node - 1)

    def qp_copy(source, target, i):
        return pltpu.make_async_remote_copy(
            src_ref=qp_all.at[source], dst_ref=qp_all.at[source],
            send_sem=qp_send.at[i], recv_sem=qp_recv.at[source],
            device_id={"db": target}, device_id_type=MESH,
        )

    def len_copy(source, target, i):
        part = len_all.at[pl.ds(source * held, held)]
        return pltpu.make_async_remote_copy(
            src_ref=part, dst_ref=part,
            send_sem=len_send.at[i], recv_sem=len_recv.at[source],
            device_id={"db": target}, device_id_type=MESH,
        )

    def res_copy(source, q, step, side):
        part = res_all.at[source * held + q]
        return pltpu.make_async_remote_copy(
            src_ref=part, dst_ref=part,
            send_sem=res_send.at[side, step, q], recv_sem=res_recv.at[source, q],
            device_id={"db": lax.rem(db + (2 * side - 1) + n, n)}, device_id_type=MESH,
        )

    def a_copy(source, owner, i):
        return pltpu.make_async_remote_copy(
            src_ref=stat.at[owner], dst_ref=stat_db.at[source],
            send_sem=a_send.at[i], recv_sem=a_recv.at[source],
            device_id={"db": owner}, device_id_type=MESH,
        )

    def b_copy(source, target, i):
        return pltpu.make_async_remote_copy(
            src_ref=stat_node.at[source], dst_ref=stat_node.at[source],
            send_sem=b_send.at[i], recv_sem=b_recv.at[source],
            device_id=target, device_id_type=MESH,
        )

    for i in range(1, n):
        qp_copy(db, on_line(i), i).start()
    local[0].wait()

    def own(side):
        for q in range(held):
            res_copy(db, q, 0, side).start()

    pl.when(db < n - 1)(lambda: own(1))
    pl.when(db > 0)(lambda: own(0))
    for i in range(1, n):
        len_copy(db, on_line(i), i).start()

    local[1].wait()
    for i in range(1, n):
        qp_copy(on_line(i), db, i).wait_recv()
    similar = lax.dot_general(
        qp_all[...].reshape(n * per_owner, width), dbp[...], (((1,), (1,)), ((), ())),
        preferred_element_type=jnp.float32,
    ) * factor
    top = jnp.max(similar, axis=1, keepdims=True)
    total = jnp.sum(jnp.exp(similar - top), axis=1, keepdims=True)
    for k in range(n):
        rows = slice(k * per_owner, (k + 1) * per_owner)
        stat[k, 0] = jnp.broadcast_to(top[rows], (per_owner, LANES))
        stat[k, 1] = jnp.broadcast_to(total[rows], (per_owner, LANES))
    for i in range(1, n):
        a_copy(db, on_line(i), i).start()
    stat_db[db] = stat[db]

    def relay(step):
        for side in (1, 0):
            source = db - step if side else db + step
            valid = source >= 0 if side else source < n
            more = db < n - 1 if side else db > 0

            @pl.when(valid)
            def _():
                for q in range(held):
                    res_copy(source, q, step, side).wait_recv()

                    @pl.when(more)
                    def _():
                        res_copy(source, q, step, side).start()

    def join_db():
        for i in range(1, n):
            a_copy(on_line(i), db, i).wait_recv()
        top, total = fold([(stat_db[k, 0], stat_db[k, 1]) for k in range(n)])
        stat_node[spot, 0] = top
        stat_node[spot, 1] = total
        for i in range(1, node):
            b_copy(spot, in_node(i)[1], i).start()

    def join_node():
        for i in range(1, node):
            b_copy(in_node(i)[0], in_node(i)[1], i).wait_recv()
        top, total = fold([(stat_node[k, 0], stat_node[k, 1]) for k in range(node)])
        coarse_ref[...] = top + jnp.log(total)

    relay(1)
    join_db()
    if n > 2:
        relay(2)
    join_node()
    if n > 3:
        lax.fori_loop(3, n, lambda step, _: (relay(step), 0)[1], 0)
    local[2].wait()
    for i in range(1, n):
        len_copy(on_line(i), db, i).wait_recv()

    def score(c, _):
        chosen = dest_ref[c, 0] * held + cq_ref[c]
        seq = seq_ref[c]
        value = align(res_all[chosen], dbres[seq], len_all[chosen][:1], dblen_ref[seq], factor)
        score_ref[pl.ds(c, 1), :] = jnp.broadcast_to(value, (1, LANES))
        return 0

    count = score_ref.shape[0]
    if count <= 8:
        for c in range(count):
            score(c, 0)
    else:
        lax.fori_loop(0, count, score, 0)

    for i in range(1, n):
        qp_copy(db, on_line(i), i).wait_send()
        len_copy(db, on_line(i), i).wait_send()
        a_copy(db, on_line(i), i).wait_send()
    for i in range(1, node):
        b_copy(spot, in_node(i)[1], i).wait_send()

    def drain(step, _):
        for side in (1, 0):
            source = db - step if side else db + step
            more = (db < n - 1) & (source >= 0) if side else (db > 0) & (source < n)

            @pl.when(more)
            def _():
                for q in range(held):
                    res_copy(source, q, step, side).wait_send()

        return 0

    lax.fori_loop(0, n, drain, 0)


def body(
    n, n_sub, n_rep,
    query_pooled, db_pooled, query_res, query_len, db_res, db_len, cand_seq, cand_dest, cand_query,
):
    per_owner, width = query_pooled.shape
    held, longest, _ = query_res.shape
    count = cand_seq.shape[0]
    node = n_sub * n_rep
    vmem, smem, anywhere = (
        pl.BlockSpec(memory_space=pltpu.VMEM),
        pl.BlockSpec(memory_space=pltpu.SMEM),
        pl.BlockSpec(memory_space=pl.ANY),
    )
    dma = pltpu.SemaphoreType.DMA
    coarse, score = pl.pallas_call(
        functools.partial(kernel, n, n_sub, n_rep),
        out_shape=(
            jax.ShapeDtypeStruct((per_owner, LANES), jnp.float32),
            jax.ShapeDtypeStruct((count, LANES), jnp.float32),
        ),
        in_specs=[vmem, anywhere, anywhere, smem, anywhere, smem, smem, smem, smem],
        out_specs=(vmem, vmem),
        scratch_shapes=[
            pltpu.VMEM((n, per_owner, width), jnp.bfloat16),
            pltpu.VMEM(db_pooled.shape, jnp.bfloat16),
            pltpu.VMEM(db_res.shape, jnp.bfloat16),
            pltpu.VMEM((n * held, longest, width), jnp.bfloat16),
            pltpu.VMEM((n * held, 8, LANES), jnp.int32),
            pltpu.VMEM((n, 2, per_owner, LANES), jnp.float32),
            pltpu.VMEM((n, 2, per_owner, LANES), jnp.float32),
            pltpu.VMEM((node, 2, per_owner, LANES), jnp.float32),
            dma((3,)),
            dma((n,)), dma((n,)), dma((n,)), dma((n,)),
            dma((2, n, held)), dma((n, held)),
            dma((n,)), dma((n,)), dma((node,)), dma((node,)),
        ],
        compiler_params=pltpu.CompilerParams(
            collective_id=0, has_side_effects=True, vmem_limit_bytes=40 * 2**20
        ),
    )(
        query_pooled, db_pooled, query_res, query_len, db_res, db_len,
        cand_seq, cand_dest, cand_query,
    )
    return coarse[:, 0], score[:, 0]


def solution(mesh):
    every = ("groups", "db", "sub", "rep")
    in_specs = (
        P(("groups", "db"), None), P(every, None), P(every, None, None), P(every),
        P(every, None, None), P(every), P(every), P(every, None), P(every),
    )
    out_specs = (P(("groups", "db")), P(every))
    sizes = [mesh.shape[a] for a in ("db", "sub", "rep")]
    return jax.shard_map(
        functools.partial(body, *sizes), mesh=mesh, in_specs=in_specs, out_specs=out_specs,
        check_vma=False,
    )
```

```python
import functools

import jax
import jax.numpy as jnp
from jax import lax
from jax.experimental import pallas as pl
from jax.experimental.pallas import tpu as pltpu
from jax.sharding import PartitionSpec as P

MESH = pl.DeviceIdType.MESH
LANES = 128


def fold(pieces):
    top = functools.reduce(jnp.maximum, [p[0] for p in pieces])
    total = sum(p[1] * jnp.exp(p[0] - top) for p in pieces)
    return top, total


def align(query, block, lq_row, lt, factor):
    similar = lax.dot_general(
        query, block, (((1,), (1,)), ((), ())), preferred_element_type=jnp.float32
    ) * factor
    rows = lax.broadcasted_iota(jnp.int32, similar.shape, 0) < lq_row[:, : similar.shape[1]]
    columns = lax.broadcasted_iota(jnp.int32, similar.shape, 1) < lt
    across = jnp.where(columns, similar, -1e30)
    weight = jnp.where(columns, jnp.exp(across - jnp.max(across, axis=1, keepdims=True)), 0.0)
    row_part = jnp.sum(weight * similar, axis=1, keepdims=True) / jnp.sum(
        weight, axis=1, keepdims=True
    )
    row_part = jnp.sum(jnp.where(rows[:, :1], row_part, 0.0), axis=0, keepdims=True)
    down = jnp.where(rows, similar, -1e30)
    weight = jnp.where(rows, jnp.exp(down - jnp.max(down, axis=0, keepdims=True)), 0.0)
    column_part = jnp.sum(weight * similar, axis=0, keepdims=True) / jnp.sum(
        weight, axis=0, keepdims=True
    )
    column_part = jnp.sum(jnp.where(columns[:1], column_part, 0.0), axis=1, keepdims=True)
    lq = lq_row[:, :1].astype(jnp.float32)
    return 0.5 * row_part / lq + 0.5 * column_part / lt.astype(jnp.float32)


def kernel(
    n, n_sub, n_rep,
    qp_ref, dbp_hbm, qres_hbm, qlen_ref, dbres_hbm, dblen_ref, seq_ref, dest_ref, cq_ref,
    coarse_ref, score_ref,
    qp_all, dbp, dbres, res_all, len_all, stat, stat_db, stat_node,
    local_sem, qp_send, qp_recv, len_send, len_recv, res_send, res_recv,
    a_send, a_recv, b_send, b_recv,
):
    db, sub, rep = lax.axis_index("db"), lax.axis_index("sub"), lax.axis_index("rep")
    node = n_sub * n_rep
    spot = sub * n_rep + rep
    per_owner, width = qp_ref.shape
    held = qres_hbm.shape[0]
    factor = width ** (-0.5)

    def on_line(i):
        return lax.rem(db + i, n)

    def in_node(i):
        other = lax.rem(spot + i, node)
        return other, {"sub": other // n_rep, "rep": lax.rem(other, n_rep)}

    local = [
        pltpu.make_async_copy(qres_hbm, res_all.at[pl.ds(db * held, held)], local_sem.at[0]),
        pltpu.make_async_copy(dbp_hbm, dbp, local_sem.at[1]),
        pltpu.make_async_copy(dbres_hbm, dbres, local_sem.at[2]),
    ]
    for copy in local:
        copy.start()
    barrier = pltpu.get_barrier_semaphore()
    for i in range(1, n):
        pl.semaphore_signal(barrier, inc=1, device_id={"db": on_line(i)}, device_id_type=MESH)
    for i in range(1, node):
        pl.semaphore_signal(barrier, inc=1, device_id=in_node(i)[1], device_id_type=MESH)
    qp_all[db] = qp_ref[...]
    for q in range(held):
        len_all[db * held + q] = jnp.full(len_all.shape[1:], qlen_ref[q], jnp.int32)
    pl.semaphore_wait(barrier, n - 1 + node - 1)

    def qp_copy(source, target, i):
        return pltpu.make_async_remote_copy(
            src_ref=qp_all.at[source], dst_ref=qp_all.at[source],
            send_sem=qp_send.at[i], recv_sem=qp_recv.at[source],
            device_id={"db": target}, device_id_type=MESH,
        )

    def len_copy(source, target, i):
        part = len_all.at[pl.ds(source * held, held)]
        return pltpu.make_async_remote_copy(
            src_ref=part, dst_ref=part,
            send_sem=len_send.at[i], recv_sem=len_recv.at[source],
            device_id={"db": target}, device_id_type=MESH,
        )

    def res_copy(source, q, step, side):
        part = res_all.at[source * held + q]
        return pltpu.make_async_remote_copy(
            src_ref=part, dst_ref=part,
            send_sem=res_send.at[side, step, q], recv_sem=res_recv.at[source, q],
            device_id={"db": lax.rem(db + (2 * side - 1) + n, n)}, device_id_type=MESH,
        )

    def a_copy(source, owner, i):
        return pltpu.make_async_remote_copy(
            src_ref=stat.at[owner], dst_ref=stat_db.at[source],
            send_sem=a_send.at[i], recv_sem=a_recv.at[source],
            device_id={"db": owner}, device_id_type=MESH,
        )

    def b_copy(source, target, i):
        return pltpu.make_async_remote_copy(
            src_ref=stat_node.at[source], dst_ref=stat_node.at[source],
            send_sem=b_send.at[i], recv_sem=b_recv.at[source],
            device_id=target, device_id_type=MESH,
        )

    for i in range(1, n):
        qp_copy(db, on_line(i), i).start()
    local[0].wait()

    def own(side):
        for q in range(held):
            res_copy(db, q, 0, side).start()

    pl.when(db < n - 1)(lambda: own(1))
    pl.when(db > 0)(lambda: own(0))
    for i in range(1, n):
        len_copy(db, on_line(i), i).start()

    local[1].wait()
    for i in range(1, n):
        qp_copy(on_line(i), db, i).wait_recv()
    similar = lax.dot_general(
        qp_all[...].reshape(n * per_owner, width), dbp[...], (((1,), (1,)), ((), ())),
        preferred_element_type=jnp.float32,
    ) * factor
    top = jnp.max(similar, axis=1, keepdims=True)
    total = jnp.sum(jnp.exp(similar - top), axis=1, keepdims=True)
    for k in range(n):
        rows = slice(k * per_owner, (k + 1) * per_owner)
        stat[k, 0] = jnp.broadcast_to(top[rows], (per_owner, LANES))
        stat[k, 1] = jnp.broadcast_to(total[rows], (per_owner, LANES))
    for i in range(1, n):
        a_copy(db, on_line(i), i).start()
    stat_db[db] = stat[db]

    def relay(step):
        for side in (1, 0):
            source = db - step if side else db + step
            valid = source >= 0 if side else source < n
            more = db < n - 1 if side else db > 0

            @pl.when(valid)
            def _():
                for q in range(held):
                    res_copy(source, q, step, side).wait_recv()

                    @pl.when(more)
                    def _():
                        res_copy(source, q, step, side).start()

    def join_db():
        for i in range(1, n):
            a_copy(on_line(i), db, i).wait_recv()
        top, total = fold([(stat_db[k, 0], stat_db[k, 1]) for k in range(n)])
        stat_node[spot, 0] = top
        stat_node[spot, 1] = total
        for i in range(1, node):
            b_copy(spot, in_node(i)[1], i).start()

    def join_node():
        for i in range(1, node):
            b_copy(in_node(i)[0], in_node(i)[1], i).wait_recv()
        top, total = fold([(stat_node[k, 0], stat_node[k, 1]) for k in range(node)])
        coarse_ref[...] = top + jnp.log(total)

    relay(1)
    join_db()
    if n > 2:
        relay(2)
    join_node()
    if n > 3:
        lax.fori_loop(3, n, lambda step, _: (relay(step), 0)[1], 0)
    local[2].wait()
    for i in range(1, n):
        len_copy(on_line(i), db, i).wait_recv()

    def score(c, _):
        chosen = dest_ref[c] * held + cq_ref[c]
        seq = seq_ref[c]
        value = align(res_all[chosen], dbres[seq], len_all[chosen][:1], dblen_ref[seq], factor)
        score_ref[pl.ds(c, 1), :] = jnp.broadcast_to(value, (1, LANES))
        return 0

    count = score_ref.shape[0]
    if count <= 8:
        for c in range(count):
            score(c, 0)
    else:
        lax.fori_loop(0, count, score, 0)

    for i in range(1, n):
        qp_copy(db, on_line(i), i).wait_send()
        len_copy(db, on_line(i), i).wait_send()
        a_copy(db, on_line(i), i).wait_send()
    for i in range(1, node):
        b_copy(spot, in_node(i)[1], i).wait_send()

    def drain(step, _):
        for side in (1, 0):
            source = db - step if side else db + step
            more = (db < n - 1) & (source >= 0) if side else (db > 0) & (source < n)

            @pl.when(more)
            def _():
                for q in range(held):
                    res_copy(source, q, step, side).wait_send()

        return 0

    lax.fori_loop(0, n, drain, 0)


def body(
    n, n_sub, n_rep,
    query_pooled, db_pooled, query_res, query_len, db_res, db_len, cand_seq, cand_dest, cand_query,
):
    per_owner, width = query_pooled.shape
    held, longest, _ = query_res.shape
    count = cand_seq.shape[0]
    node = n_sub * n_rep
    vmem, smem, anywhere = (
        pl.BlockSpec(memory_space=pltpu.VMEM),
        pl.BlockSpec(memory_space=pltpu.SMEM),
        pl.BlockSpec(memory_space=pltpu.HBM),
    )
    dma = pltpu.SemaphoreType.DMA
    coarse, score = pl.pallas_call(
        functools.partial(kernel, n, n_sub, n_rep),
        out_shape=(
            jax.ShapeDtypeStruct((per_owner, LANES), jnp.float32),
            jax.ShapeDtypeStruct((count, LANES), jnp.float32),
        ),
        in_specs=[vmem, anywhere, anywhere, smem, anywhere, smem, smem, smem, smem],
        out_specs=(vmem, vmem),
        scratch_shapes=[
            pltpu.VMEM((n, per_owner, width), jnp.bfloat16),
            pltpu.VMEM(db_pooled.shape, jnp.bfloat16),
            pltpu.VMEM(db_res.shape, jnp.bfloat16),
            pltpu.VMEM((n * held, longest, width), jnp.bfloat16),
            pltpu.VMEM((n * held, 8, LANES), jnp.int32),
            pltpu.VMEM((n, 2, per_owner, LANES), jnp.float32),
            pltpu.VMEM((n, 2, per_owner, LANES), jnp.float32),
            pltpu.VMEM((node, 2, per_owner, LANES), jnp.float32),
            dma((3,)),
            dma((n,)), dma((n,)), dma((n,)), dma((n,)),
            dma((2, n, held)), dma((n, held)),
            dma((n,)), dma((n,)), dma((node,)), dma((node,)),
        ],
        compiler_params=pltpu.CompilerParams(
            collective_id=0, has_side_effects=True, vmem_limit_bytes=60 * 2**20
        ),
    )(
        query_pooled, db_pooled, query_res, query_len, db_res, db_len,
        cand_seq, cand_dest[:, 0], cand_query,
    )
    return coarse[:, 0], score[:, 0]


def solution(mesh):
    every = ("groups", "db", "sub", "rep")
    in_specs = (
        P(("groups", "db"), None), P(every, None), P(every, None, None), P(every),
        P(every, None, None), P(every), P(every), P(every, None), P(every),
    )
    out_specs = (P(("groups", "db")), P(every))
    sizes = [mesh.shape[a] for a in ("db", "sub", "rep")]
    return jax.shard_map(
        functools.partial(body, *sizes), mesh=mesh, in_specs=in_specs, out_specs=out_specs,
        check_vma=False,
    )
```

```python
import functools

import jax
import jax.numpy as jnp
from jax import lax
from jax.experimental import pallas as pl
from jax.experimental.pallas import tpu as pltpu
from jax.sharding import PartitionSpec as P

MESH = pl.DeviceIdType.MESH
LANES = 128


def fold(pieces):
    top = functools.reduce(jnp.maximum, [p[0] for p in pieces])
    total = sum(p[1] * jnp.exp(p[0] - top) for p in pieces)
    return top, total


def align(query, block, lq_row, lt, factor):
    similar = lax.dot_general(
        query, block, (((1,), (1,)), ((), ())), preferred_element_type=jnp.float32
    ) * factor
    rows = lax.broadcasted_iota(jnp.int32, similar.shape, 0) < lq_row[:, : similar.shape[1]]
    columns = lax.broadcasted_iota(jnp.int32, similar.shape, 1) < lt
    across = jnp.where(columns, similar, -1e30)
    weight = jnp.where(columns, jnp.exp(across - jnp.max(across, axis=1, keepdims=True)), 0.0)
    row_part = jnp.sum(weight * similar, axis=1, keepdims=True) / jnp.sum(
        weight, axis=1, keepdims=True
    )
    row_part = jnp.sum(jnp.where(rows[:, :1], row_part, 0.0), axis=0, keepdims=True)
    down = jnp.where(rows, similar, -1e30)
    weight = jnp.where(rows, jnp.exp(down - jnp.max(down, axis=0, keepdims=True)), 0.0)
    column_part = jnp.sum(weight * similar, axis=0, keepdims=True) / jnp.sum(
        weight, axis=0, keepdims=True
    )
    column_part = jnp.sum(jnp.where(columns[:1], column_part, 0.0), axis=1, keepdims=True)
    lq = lq_row[:, :1].astype(jnp.float32)
    return 0.5 * row_part / lq + 0.5 * column_part / lt.astype(jnp.float32)


def kernel(
    n, n_sub, n_rep,
    qp_ref, dbp_hbm, qres_hbm, qlen_ref, dbres_hbm, dblen_ref, seq_ref, dest_ref, cq_ref,
    coarse_ref, score_ref,
    qp_all, dbp, dbres, res_all, len_all, stat, stat_db, stat_node,
    local_sem, qp_send, qp_recv, len_send, len_recv, res_send, res_recv,
    a_send, a_recv, b_send, b_recv, share_send, share_recv,
):
    db, sub, rep = lax.axis_index("db"), lax.axis_index("sub"), lax.axis_index("rep")
    node = n_sub * n_rep
    spot = sub * n_rep + rep
    per_owner, width = qp_ref.shape
    held = qres_hbm.shape[0]
    factor = width ** (-0.5)

    def on_line(i):
        return lax.rem(db + i, n)

    def in_node(i):
        other = lax.rem(spot + i, node)
        return other, {"sub": other // n_rep, "rep": lax.rem(other, n_rep)}

    local = [
        pltpu.make_async_copy(qres_hbm, res_all.at[pl.ds(db * held, held)], local_sem.at[0]),
        pltpu.make_async_copy(dbp_hbm, dbp, local_sem.at[1]),
        pltpu.make_async_copy(dbres_hbm, dbres, local_sem.at[2]),
    ]
    for copy in local:
        copy.start()
    barrier = pltpu.get_barrier_semaphore()
    for i in range(1, n):
        pl.semaphore_signal(barrier, inc=1, device_id={"db": on_line(i)}, device_id_type=MESH)
    for i in range(1, node):
        pl.semaphore_signal(barrier, inc=1, device_id=in_node(i)[1], device_id_type=MESH)
    qp_all[db] = qp_ref[...]
    for q in range(held):
        len_all[db * held + q] = jnp.full(len_all.shape[1:], qlen_ref[q], jnp.int32)
    pl.semaphore_wait(barrier, n - 1 + node - 1)

    half = width // n_rep

    def columns(core):
        return pl.ds(pl.multiple_of(core * half, LANES), half)

    def qp_copy(source, target, i):
        part = qp_all.at[source, :, columns(rep)]
        return pltpu.make_async_remote_copy(
            src_ref=part, dst_ref=part,
            send_sem=qp_send.at[i], recv_sem=qp_recv.at[source],
            device_id={"db": target}, device_id_type=MESH,
        )

    def share_copy(source, core, i):
        part = qp_all.at[source, :, columns(core)]
        return pltpu.make_async_remote_copy(
            src_ref=part, dst_ref=part,
            send_sem=share_send.at[i], recv_sem=share_recv.at[source],
            device_id={"rep": 1 - rep}, device_id_type=MESH,
        )

    def len_copy(source, target, i):
        part = len_all.at[pl.ds(source * held, held)]
        return pltpu.make_async_remote_copy(
            src_ref=part, dst_ref=part,
            send_sem=len_send.at[i], recv_sem=len_recv.at[source],
            device_id={"db": target}, device_id_type=MESH,
        )

    def res_copy(source, q, step, side):
        part = res_all.at[source * held + q]
        return pltpu.make_async_remote_copy(
            src_ref=part, dst_ref=part,
            send_sem=res_send.at[side, step, q], recv_sem=res_recv.at[source, q],
            device_id={"db": lax.rem(db + (2 * side - 1) + n, n)}, device_id_type=MESH,
        )

    def a_copy(source, owner, i):
        return pltpu.make_async_remote_copy(
            src_ref=stat.at[owner], dst_ref=stat_db.at[source],
            send_sem=a_send.at[i], recv_sem=a_recv.at[source],
            device_id={"db": owner}, device_id_type=MESH,
        )

    def b_copy(source, target, i):
        return pltpu.make_async_remote_copy(
            src_ref=stat_node.at[source], dst_ref=stat_node.at[source],
            send_sem=b_send.at[i], recv_sem=b_recv.at[source],
            device_id=target, device_id_type=MESH,
        )

    for i in range(1, n):
        qp_copy(db, on_line(i), i).start()
    local[0].wait()

    def own(side):
        for q in range(held):
            res_copy(db, q, 0, side).start()

    pl.when(db < n - 1)(lambda: own(1))
    pl.when(db > 0)(lambda: own(0))
    for i in range(1, n):
        len_copy(db, on_line(i), i).start()

    local[1].wait()
    for i in range(1, n):
        qp_copy(on_line(i), db, i).wait_recv()
        share_copy(on_line(i), rep, i).start()
    for i in range(1, n):
        share_copy(on_line(i), 1 - rep, i).wait_recv()
    similar = lax.dot_general(
        qp_all[...].reshape(n * per_owner, width), dbp[...], (((1,), (1,)), ((), ())),
        preferred_element_type=jnp.float32,
    ) * factor
    top = jnp.max(similar, axis=1, keepdims=True)
    total = jnp.sum(jnp.exp(similar - top), axis=1, keepdims=True)
    for k in range(n):
        rows = slice(k * per_owner, (k + 1) * per_owner)
        stat[k, 0] = jnp.broadcast_to(top[rows], (per_owner, LANES))
        stat[k, 1] = jnp.broadcast_to(total[rows], (per_owner, LANES))
    for i in range(1, n):
        a_copy(db, on_line(i), i).start()
    stat_db[db] = stat[db]

    def relay(step):
        for side in (1, 0):
            source = db - step if side else db + step
            valid = source >= 0 if side else source < n
            more = db < n - 1 if side else db > 0

            @pl.when(valid)
            def _():
                for q in range(held):
                    res_copy(source, q, step, side).wait_recv()

                    @pl.when(more)
                    def _():
                        res_copy(source, q, step, side).start()

    def join_db():
        for i in range(1, n):
            a_copy(on_line(i), db, i).wait_recv()
        top, total = fold([(stat_db[k, 0], stat_db[k, 1]) for k in range(n)])
        stat_node[spot, 0] = top
        stat_node[spot, 1] = total
        for i in range(1, node):
            b_copy(spot, in_node(i)[1], i).start()

    def join_node():
        for i in range(1, node):
            b_copy(in_node(i)[0], in_node(i)[1], i).wait_recv()
        top, total = fold([(stat_node[k, 0], stat_node[k, 1]) for k in range(node)])
        coarse_ref[...] = top + jnp.log(total)

    relay(1)
    join_db()
    if n > 2:
        relay(2)
    join_node()
    if n > 3:
        lax.fori_loop(3, n, lambda step, _: (relay(step), 0)[1], 0)
    local[2].wait()
    for i in range(1, n):
        len_copy(on_line(i), db, i).wait_recv()

    def score(c, _):
        chosen = dest_ref[c] * held + cq_ref[c]
        seq = seq_ref[c]
        value = align(res_all[chosen], dbres[seq], len_all[chosen][:1], dblen_ref[seq], factor)
        score_ref[pl.ds(c, 1), :] = jnp.broadcast_to(value, (1, LANES))
        return 0

    count = score_ref.shape[0]
    if count <= 8:
        for c in range(count):
            score(c, 0)
    else:
        lax.fori_loop(0, count, score, 0)

    for i in range(1, n):
        qp_copy(db, on_line(i), i).wait_send()
        share_copy(on_line(i), rep, i).wait_send()
        len_copy(db, on_line(i), i).wait_send()
        a_copy(db, on_line(i), i).wait_send()
    for i in range(1, node):
        b_copy(spot, in_node(i)[1], i).wait_send()

    def drain(step, _):
        for side in (1, 0):
            source = db - step if side else db + step
            more = (db < n - 1) & (source >= 0) if side else (db > 0) & (source < n)

            @pl.when(more)
            def _():
                for q in range(held):
                    res_copy(source, q, step, side).wait_send()

        return 0

    lax.fori_loop(0, n, drain, 0)


def body(
    n, n_sub, n_rep,
    query_pooled, db_pooled, query_res, query_len, db_res, db_len, cand_seq, cand_dest, cand_query,
):
    per_owner, width = query_pooled.shape
    held, longest, _ = query_res.shape
    count = cand_seq.shape[0]
    node = n_sub * n_rep
    vmem, smem, anywhere = (
        pl.BlockSpec(memory_space=pltpu.VMEM),
        pl.BlockSpec(memory_space=pltpu.SMEM),
        pl.BlockSpec(memory_space=pltpu.HBM),
    )
    dma = pltpu.SemaphoreType.DMA
    coarse, score = pl.pallas_call(
        functools.partial(kernel, n, n_sub, n_rep),
        out_shape=(
            jax.ShapeDtypeStruct((per_owner, LANES), jnp.float32),
            jax.ShapeDtypeStruct((count, LANES), jnp.float32),
        ),
        in_specs=[vmem, anywhere, anywhere, smem, anywhere, smem, smem, smem, smem],
        out_specs=(vmem, vmem),
        scratch_shapes=[
            pltpu.VMEM((n, per_owner, width), jnp.bfloat16),
            pltpu.VMEM(db_pooled.shape, jnp.bfloat16),
            pltpu.VMEM(db_res.shape, jnp.bfloat16),
            pltpu.VMEM((n * held, longest, width), jnp.bfloat16),
            pltpu.VMEM((n * held, 8, LANES), jnp.int32),
            pltpu.VMEM((n, 2, per_owner, LANES), jnp.float32),
            pltpu.VMEM((n, 2, per_owner, LANES), jnp.float32),
            pltpu.VMEM((node, 2, per_owner, LANES), jnp.float32),
            dma((3,)),
            dma((n,)), dma((n,)), dma((n,)), dma((n,)),
            dma((2, n, held)), dma((n, held)),
            dma((n,)), dma((n,)), dma((node,)), dma((node,)), dma((n,)), dma((n,)),
        ],
        compiler_params=pltpu.CompilerParams(
            collective_id=0, has_side_effects=True, vmem_limit_bytes=60 * 2**20
        ),
    )(
        query_pooled, db_pooled, query_res, query_len, db_res, db_len,
        cand_seq, cand_dest[:, 0], cand_query,
    )
    return coarse[:, 0], score[:, 0]


def solution(mesh):
    every = ("groups", "db", "sub", "rep")
    in_specs = (
        P(("groups", "db"), None), P(every, None), P(every, None, None), P(every),
        P(every, None, None), P(every), P(every), P(every, None), P(every),
    )
    out_specs = (P(("groups", "db")), P(every))
    sizes = [mesh.shape[a] for a in ("db", "sub", "rep")]
    return jax.shard_map(
        functools.partial(body, *sizes), mesh=mesh, in_specs=in_specs, out_specs=out_specs,
        check_vma=False,
    )
```

```python
import functools

import jax
import jax.numpy as jnp
from jax import lax
from jax.experimental import pallas as pl
from jax.experimental.pallas import tpu as pltpu
from jax.sharding import PartitionSpec as P

MESH = pl.DeviceIdType.MESH
LANES = 128


def fold(pieces):
    top = functools.reduce(jnp.maximum, [p[0] for p in pieces])
    total = sum(p[1] * jnp.exp(p[0] - top) for p in pieces)
    return top, total


def align(query, block, lq_row, lt, factor):
    similar = lax.dot_general(
        query, block, (((1,), (1,)), ((), ())), preferred_element_type=jnp.float32
    ) * factor
    rows = lax.broadcasted_iota(jnp.int32, similar.shape, 0) < lq_row[:, : similar.shape[1]]
    columns = lax.broadcasted_iota(jnp.int32, similar.shape, 1) < lt
    across = jnp.where(columns, similar, -1e30)
    weight = jnp.where(columns, jnp.exp(across - jnp.max(across, axis=1, keepdims=True)), 0.0)
    row_part = jnp.sum(weight * similar, axis=1, keepdims=True) / jnp.sum(
        weight, axis=1, keepdims=True
    )
    row_part = jnp.sum(jnp.where(rows[:, :1], row_part, 0.0), axis=0, keepdims=True)
    down = jnp.where(rows, similar, -1e30)
    weight = jnp.where(rows, jnp.exp(down - jnp.max(down, axis=0, keepdims=True)), 0.0)
    column_part = jnp.sum(weight * similar, axis=0, keepdims=True) / jnp.sum(
        weight, axis=0, keepdims=True
    )
    column_part = jnp.sum(jnp.where(columns[:1], column_part, 0.0), axis=1, keepdims=True)
    lq = lq_row[:, :1].astype(jnp.float32)
    return 0.5 * row_part / lq + 0.5 * column_part / lt.astype(jnp.float32)


def kernel(
    n, n_sub, n_rep,
    qp_ref, dbp_hbm, qres_hbm, qlen_ref, dbres_hbm, dblen_ref, seq_ref, dest_ref, cq_ref,
    coarse_ref, score_ref,
    qp_all, dbp, dbres, res_all, len_all, stat, stat_db, stat_node,
    local_sem, qp_send, qp_recv, len_send, len_recv, res_send, res_recv,
    a_send, a_recv, b_send, b_recv, share_send, share_recv,
):
    db, sub, rep = lax.axis_index("db"), lax.axis_index("sub"), lax.axis_index("rep")
    node = n_sub * n_rep
    spot = sub * n_rep + rep
    per_owner, width = qp_ref.shape
    held = qres_hbm.shape[0]
    factor = width ** (-0.5)

    def on_line(i):
        return lax.rem(db + i, n)

    def in_node(i):
        other = lax.rem(spot + i, node)
        return other, {"sub": other // n_rep, "rep": lax.rem(other, n_rep)}

    local = [
        pltpu.make_async_copy(qres_hbm, res_all.at[pl.ds(db * held, held)], local_sem.at[0]),
        pltpu.make_async_copy(dbp_hbm, dbp, local_sem.at[1]),
        pltpu.make_async_copy(dbres_hbm, dbres, local_sem.at[2]),
    ]
    for copy in local:
        copy.start()
    barrier = pltpu.get_barrier_semaphore()
    for i in range(1, n):
        pl.semaphore_signal(barrier, inc=1, device_id={"db": on_line(i)}, device_id_type=MESH)
    for i in range(1, node):
        pl.semaphore_signal(barrier, inc=1, device_id=in_node(i)[1], device_id_type=MESH)
    qp_all[db] = qp_ref[...]
    for q in range(held):
        len_all[db * held + q] = jnp.full(len_all.shape[1:], qlen_ref[q], jnp.int32)
    pl.semaphore_wait(barrier, n - 1 + node - 1)

    half = width // n_rep

    def columns(core):
        return pl.ds(pl.multiple_of(core * half, LANES), half)

    def qp_copy(source, target, i):
        part = qp_all.at[source, :, columns(rep)]
        return pltpu.make_async_remote_copy(
            src_ref=part, dst_ref=part,
            send_sem=qp_send.at[i], recv_sem=qp_recv.at[source],
            device_id={"db": target}, device_id_type=MESH,
        )

    def share_copy(source, core, i):
        part = qp_all.at[source, :, columns(core)]
        return pltpu.make_async_remote_copy(
            src_ref=part, dst_ref=part,
            send_sem=share_send.at[i], recv_sem=share_recv.at[source],
            device_id={"rep": 1 - rep}, device_id_type=MESH,
        )

    def len_copy(source, target, i):
        part = len_all.at[pl.ds(source * held, held)]
        return pltpu.make_async_remote_copy(
            src_ref=part, dst_ref=part,
            send_sem=len_send.at[i], recv_sem=len_recv.at[source],
            device_id={"db": target}, device_id_type=MESH,
        )

    def res_copy(source, q, step, side):
        part = res_all.at[source * held + q]
        return pltpu.make_async_remote_copy(
            src_ref=part, dst_ref=part,
            send_sem=res_send.at[side, step, q], recv_sem=res_recv.at[source, q],
            device_id={"db": lax.rem(db + (2 * side - 1) + n, n)}, device_id_type=MESH,
        )

    def a_copy(source, owner, i):
        return pltpu.make_async_remote_copy(
            src_ref=stat.at[owner], dst_ref=stat_db.at[source],
            send_sem=a_send.at[i], recv_sem=a_recv.at[source],
            device_id={"db": owner}, device_id_type=MESH,
        )

    def b_copy(source, target, i):
        return pltpu.make_async_remote_copy(
            src_ref=stat_node.at[source], dst_ref=stat_node.at[source],
            send_sem=b_send.at[i], recv_sem=b_recv.at[source],
            device_id=target, device_id_type=MESH,
        )

    for i in range(1, n):
        qp_copy(db, on_line(i), i).start()
    local[0].wait()

    def own(side):
        for q in range(held):
            res_copy(db, q, 0, side).start()

    pl.when(db < n - 1)(lambda: own(1))
    pl.when(db > 0)(lambda: own(0))
    for i in range(1, n):
        len_copy(db, on_line(i), i).start()

    local[1].wait()
    for i in range(1, n):
        qp_copy(on_line(i), db, i).wait_recv()
        share_copy(on_line(i), rep, i).start()
    for i in range(1, n):
        share_copy(on_line(i), 1 - rep, i).wait_recv()
    similar = lax.dot_general(
        qp_all[...].reshape(n * per_owner, width), dbp[...], (((1,), (1,)), ((), ())),
        preferred_element_type=jnp.float32,
    ) * factor
    top = jnp.max(similar, axis=1, keepdims=True)
    total = jnp.sum(jnp.exp(similar - top), axis=1, keepdims=True)
    for k in range(n):
        rows = slice(k * per_owner, (k + 1) * per_owner)
        stat[k, 0] = jnp.broadcast_to(top[rows], (per_owner, LANES))
        stat[k, 1] = jnp.broadcast_to(total[rows], (per_owner, LANES))
    for i in range(1, n):
        a_copy(db, on_line(i), i).start()
    stat_db[db] = stat[db]

    def relay(step):
        for side in (1, 0):
            source = db - step if side else db + step
            valid = source >= 0 if side else source < n
            more = db < n - 1 if side else db > 0

            @pl.when(valid)
            def _():
                for q in range(held):
                    res_copy(source, q, step, side).wait_recv()

                    @pl.when(more)
                    def _():
                        res_copy(source, q, step, side).start()

    def join_db():
        for i in range(1, n):
            a_copy(on_line(i), db, i).wait_recv()
        top, total = fold([(stat_db[k, 0], stat_db[k, 1]) for k in range(n)])
        stat_node[spot, 0] = top
        stat_node[spot, 1] = total
        for i in range(1, node):
            b_copy(spot, in_node(i)[1], i).start()

    def join_node():
        for i in range(1, node):
            b_copy(in_node(i)[0], in_node(i)[1], i).wait_recv()
        top, total = fold([(stat_node[k, 0], stat_node[k, 1]) for k in range(node)])
        value = top + jnp.log(total)
        square = [lax.broadcasted_iota(jnp.int32, value.shape, d) for d in range(2)]
        value = jnp.sum(jnp.where(square[0] == square[1], value, 0.0), axis=0, keepdims=True)
        coarse_ref[...] = value[:, :per_owner]

    relay(1)
    if n > 2:
        relay(2)
    join_db()
    join_node()
    if n > 3:
        lax.fori_loop(3, n, lambda step, _: (relay(step), 0)[1], 0)
    local[2].wait()
    for i in range(1, n):
        len_copy(on_line(i), db, i).wait_recv()

    def score(c, _):
        chosen = dest_ref[c] * held + cq_ref[c]
        seq = seq_ref[c]
        value = align(res_all[chosen], dbres[seq], len_all[chosen][:1], dblen_ref[seq], factor)
        lane = lax.broadcasted_iota(jnp.int32, score_ref.shape, 1)
        score_ref[...] = jnp.where(lane == c, value, score_ref[...])
        return 0

    count = score_ref.shape[1]
    score_ref[...] = jnp.zeros_like(score_ref)
    if count <= 8:
        for c in range(count):
            score(c, 0)
    else:
        lax.fori_loop(0, count, score, 0)

    for i in range(1, n):
        qp_copy(db, on_line(i), i).wait_send()
        share_copy(on_line(i), rep, i).wait_send()
        len_copy(db, on_line(i), i).wait_send()
        a_copy(db, on_line(i), i).wait_send()
    for i in range(1, node):
        b_copy(spot, in_node(i)[1], i).wait_send()

    def drain(step, _):
        for side in (1, 0):
            source = db - step if side else db + step
            more = (db < n - 1) & (source >= 0) if side else (db > 0) & (source < n)

            @pl.when(more)
            def _():
                for q in range(held):
                    res_copy(source, q, step, side).wait_send()

        return 0

    lax.fori_loop(0, n, drain, 0)


def body(
    n, n_sub, n_rep,
    query_pooled, db_pooled, query_res, query_len, db_res, db_len, cand_seq, cand_dest, cand_query,
):
    per_owner, width = query_pooled.shape
    held, longest, _ = query_res.shape
    count = cand_seq.shape[0]
    node = n_sub * n_rep
    vmem, smem, anywhere = (
        pl.BlockSpec(memory_space=pltpu.VMEM),
        pl.BlockSpec(memory_space=pltpu.SMEM),
        pl.BlockSpec(memory_space=pltpu.HBM),
    )
    dma = pltpu.SemaphoreType.DMA
    coarse, score = pl.pallas_call(
        functools.partial(kernel, n, n_sub, n_rep),
        out_shape=(
            jax.ShapeDtypeStruct((1, per_owner), jnp.float32),
            jax.ShapeDtypeStruct((1, count), jnp.float32),
        ),
        in_specs=[vmem, anywhere, anywhere, smem, anywhere, smem, smem, smem, smem],
        out_specs=(vmem, vmem),
        scratch_shapes=[
            pltpu.VMEM((n, per_owner, width), jnp.bfloat16),
            pltpu.VMEM(db_pooled.shape, jnp.bfloat16),
            pltpu.VMEM(db_res.shape, jnp.bfloat16),
            pltpu.VMEM((n * held, longest, width), jnp.bfloat16),
            pltpu.VMEM((n * held, 8, LANES), jnp.int32),
            pltpu.VMEM((n, 2, per_owner, LANES), jnp.float32),
            pltpu.VMEM((n, 2, per_owner, LANES), jnp.float32),
            pltpu.VMEM((node, 2, per_owner, LANES), jnp.float32),
            dma((3,)),
            dma((n,)), dma((n,)), dma((n,)), dma((n,)),
            dma((2, n, held)), dma((n, held)),
            dma((n,)), dma((n,)), dma((node,)), dma((node,)), dma((n,)), dma((n,)),
        ],
        compiler_params=pltpu.CompilerParams(
            collective_id=0, has_side_effects=True, vmem_limit_bytes=60 * 2**20
        ),
    )(
        query_pooled, db_pooled, query_res, query_len, db_res, db_len,
        cand_seq, cand_dest[:, 0], cand_query,
    )
    return coarse[0], score[0]


def solution(mesh):
    every = ("groups", "db", "sub", "rep")
    in_specs = (
        P(("groups", "db"), None), P(every, None), P(every, None, None), P(every),
        P(every, None, None), P(every), P(every), P(every, None), P(every),
    )
    out_specs = (P(("groups", "db")), P(every))
    sizes = [mesh.shape[a] for a in ("db", "sub", "rep")]
    return jax.shard_map(
        functools.partial(body, *sizes), mesh=mesh, in_specs=in_specs, out_specs=out_specs,
        check_vma=False,
    )
```
